256 devices in a mesh: layer: 4 (over y_lo, core), dp: 64 (over x, z, y_hi).
Axes of the slice: x: 4, y: 4 (y_hi: 2, y_lo: 2; y = y_hi * 2 + y_lo), z: 8, core: 2. Of those that a mesh axis runs over, the one named last changes fastest.
Arguments:
- gradients: bfloat16 [32768, 8, 4096], P('dp', 'layer'), may hold values from -6 to 6
- whitener: bfloat16 [8, 16, 256, 256], P('layer')
- owners: int32 [2], replicated, may hold values from 0 to 63
- query_ids: int32 [2, 64], replicated, may hold values from 0 to 511
Outputs:
- scores: float32 [128, 32768], P('layer', 'dp')
The draws below stay inside these ranges and needn't reach their ends.
All inputs are finite; a program needn't handle non-finite values.
Results may differ from the reference program's by a relative error of at most 0.0029.
Values may be sent and summed in bfloat16 or wider, within the bound.
No kernel may reach another device: no remote copies, remote signals or barrier semaphores. Data moves between devices by JAX's collectives and lax.ppermute only.
A program may use at most 128 MiB of HBM per device.

```python
import jax
import jax.numpy as jnp
from jax import lax

PROJ = 4096
BLOCK = 256
EX_DEV = 512
QUERIES = 64
ROUNDS = 2
LAYERS = 8
EXAMPLES = 32768
N_DP = 64


def draw_whitener(key, part):
    key = jax.random.fold_in(key, 7)
    nblock = PROJ // BLOCK
    shape = (LAYERS, nblock, BLOCK, BLOCK)
    key_off, key_diag = jax.random.split(key)
    off = jax.random.normal(key_off, shape, jnp.float32) * 0.7 / BLOCK ** 0.5
    diag = jax.random.uniform(key_diag, shape, jnp.float32, 1.0, 2.0)
    rowpos = jax.lax.broadcasted_iota(jnp.int32, shape, 2)
    colpos = jax.lax.broadcasted_iota(jnp.int32, shape, 3)
    layerpos = jax.lax.broadcasted_iota(jnp.int32, shape, 0).astype(jnp.float32)
    lscale = 1.0 + 2.0 * layerpos / max(LAYERS - 1, 1)
    full = jnp.where(rowpos == colpos, diag, off) * lscale
    return full.astype(jnp.bfloat16)


def touch_ends(result, own_key, least, largest):
    longest = result.shape.index(max(result.shape))
    spots = []
    for shift in (0, 1):
        where = [jax.random.randint(jax.random.fold_in(own_key, axis), (), 0, length) for axis, length in enumerate(result.shape)]
        where[longest] = (where[longest] + shift) % result.shape[longest]
        spots.append(tuple(where))
    return result.at[spots[0]].set(least).at[spots[1]].set(largest)


def level_of(rng, extent, shards, smallest, high):
    def one(dim, blocks):
        heights = jax.random.uniform(jax.random.fold_in(jax.random.fold_in(rng, 6), dim), (blocks,), jnp.float32, smallest / len(shards), high / len(shards))
        return jnp.repeat(jnp.exp(heights), extent[dim] // blocks).reshape((-1,) + (1,) * (len(extent) - dim - 1))

    gain = one(*shards[0])
    for cut in shards[1:]:
        gain = gain * one(*cut)
    return gain


def scatter_about(stream_key, shape, spread, bound, shards=(), dtype=jnp.bfloat16):
    result = spread * jax.random.normal(stream_key, shape, jnp.float32)
    if shards:
        result = result * level_of(stream_key, shape, shards, -0.22, 0.18)
    return jnp.clip(result, -bound, bound).astype(dtype)


def setup_inputs(seed: int = 0) -> dict:
    seeds = jax.random.split(jax.random.key(seed), 5)
    gradients = scatter_about(seeds[0], (EXAMPLES, LAYERS, PROJ), 1.0, 6.0, ((0, 64), (1, 4)))
    whitener = draw_whitener(jax.random.fold_in(seeds[4], 71), 0)
    owners = jax.random.randint(seeds[2], (ROUNDS,), 0, N_DP).astype(jnp.int32)
    query_ids = touch_ends(jax.random.randint(seeds[3], (ROUNDS, QUERIES), 0, EX_DEV), jax.random.fold_in(seeds[3], 1), 0, EX_DEV - 1).astype(jnp.int32)
    return dict(gradients=gradients, whitener=whitener, owners=owners, query_ids=query_ids)


def reference(gradients, whitener, owners, query_ids):
    total = gradients.shape[0]
    nblock = PROJ // BLOCK
    rows = (owners[:, None] * EX_DEV + query_ids).reshape(-1).astype(jnp.int32)
    layer_major = jnp.moveaxis(gradients, 1, 0)

    def one_layer(carry, inputs):
        acc, norms = carry
        grad_layer, white_map = inputs
        split = grad_layer.reshape(total, nblock, BLOCK).astype(jnp.float32)
        whitened = jnp.einsum('ebj,bij->ebi', split, white_map.astype(jnp.float32)).reshape(total, PROJ)
        norms = norms + lax.optimization_barrier(jnp.sum(whitened * whitened, axis=1))
        white_rows = whitened.astype(jnp.bfloat16)
        query = jnp.take(white_rows, rows, axis=0)
        acc = acc + lax.dot_general(query, white_rows, (((1,), (1,)), ((), ())), preferred_element_type=jnp.float32)
        return ((acc, norms), None)
    start = (jnp.zeros((ROUNDS * QUERIES, total), jnp.float32), jnp.zeros((total,), jnp.float32))
    (acc, norms), unused = lax.scan(one_layer, start, (layer_major, whitener))
    return acc / jnp.sqrt(norms + 1e-06)[None, :]
```

```python
import functools
import itertools

import jax
import jax.numpy as jnp
from jax import lax
from jax.experimental import pallas as pl
from jax.experimental.pallas import tpu as pltpu
from jax.sharding import Mesh
from jax.sharding import PartitionSpec as P

NX, NZ, NY = 4, 8, 2
DP = ("x", "z", "yhi")
LAYER = ("ylo", "core")
AXES = LAYER + DP
SIZES = dict(x=NX, z=NZ, yhi=NY)


def shift(value, dx=0, dz=0, dy=0):
    moves = {name: by for name, by in (("x", dx), ("z", dz), ("yhi", dy)) if by}
    names = tuple(moves)

    def index(place):
        flat = 0
        for name, at in zip(names, place):
            flat = flat * SIZES[name] + at % SIZES[name]
        return flat

    pairs = [
        (index(place), index([at + moves[name] for name, at in zip(names, place)]))
        for place in itertools.product(*(range(SIZES[name]) for name in names))
    ]
    return lax.ppermute(value, names if len(names) > 1 else names[0], pairs)


def pick_kernel(counts, ids, gradients, *rest):
    outs, sem = rest[:-1], rest[-1]
    total = 0
    for out, count in zip(outs, counts):
        base = total

        def start(row, carry, out=out, base=base):
            pltpu.make_async_copy(
                gradients.at[ids[base + row]], out.at[row], sem
            ).start()
            return carry

        lax.fori_loop(0, count, start, 0, unroll=8)
        total += count
    for out, count in zip(outs, counts):
        pltpu.make_async_copy(gradients.at[pl.ds(0, count)], out, sem).wait()


def pick_rows(gradients, ids, counts):
    row = gradients.shape[1:]
    moved = 2 * sum(counts) * row[0] * row[1] * gradients.dtype.itemsize
    return pl.pallas_call(
        functools.partial(pick_kernel, counts),
        out_shape=[jax.ShapeDtypeStruct((n,) + row, gradients.dtype) for n in counts],
        in_specs=[
            pl.BlockSpec(memory_space=pltpu.SMEM),
            pl.BlockSpec(memory_space=pl.ANY),
        ],
        out_specs=[pl.BlockSpec(memory_space=pl.ANY) for _ in counts],
        scratch_shapes=[pltpu.SemaphoreType.DMA],
        cost_estimate=pl.CostEstimate(flops=0, bytes_accessed=moved, transcendentals=0),
    )(ids, gradients)


def per_round(flag):
    return flag.reshape(-1, 1, 1, 1)


def piece(parts, at):
    return lax.dynamic_index_in_dim(parts, at, 1, keepdims=False)


def broadcast(gradients, owners, query_ids):
    rounds, queries = query_ids.shape
    tail = gradients.shape[1:]
    quarter, part = queries // 4, queries // 16
    x, z, y = (lax.axis_index(name) for name in DP)
    colour = (x + 2 * z) % 4
    own_x, own_z, own_y = owners // (NZ * NY), owners // NY % NZ, owners % NY
    far_x, far_z, same_y = (x - own_x) % NX, (z - own_z) % NZ, y == own_y

    by_colour = query_ids.reshape(rounds, 4, quarter)
    order = [by_colour[:, (colour + turn) % 4].reshape(-1) for turn in (0, 1, 3)]
    across = by_colour[:, (colour + 2) % 4]
    order += [across[:, : quarter // 2].reshape(-1), across[:, quarter // 2 :].reshape(-1)]
    counts = tuple(ids.shape[0] for ids in order)
    own, to_right, to_left, to_up, to_down = pick_rows(
        gradients, jnp.concatenate(order), counts
    )
    from_left = shift(to_right, dx=1).reshape(rounds, 4, part, *tail)
    from_right = shift(to_left, dx=-1).reshape(rounds, 4, part, *tail)
    from_below = shift(to_up, dz=1).reshape(rounds, 2, part, *tail)
    from_above = shift(to_down, dz=-1).reshape(rounds, 2, part, *tail)
    own = own.reshape(rounds, 4, part, *tail)

    def held(at):
        low = at < 2
        out = piece(own, at)
        out = jnp.where(per_round((far_x == 0) & (far_z == 1) & low), piece(from_below, at % 2), out)
        out = jnp.where(per_round((far_x == 0) & (far_z == 7) & ~low), piece(from_above, at % 2), out)
        out = jnp.where(per_round((far_x == 1) & (far_z == 0)), piece(from_left, at), out)
        return jnp.where(per_round((far_x == 3) & (far_z == 0)), piece(from_right, at), out)

    mine = z % 4
    got = {0: held(mine)}
    for by in (1, 2, -1):
        got[by] = shift(held((z + by) % 4), dx=(-2 * by) % 4, dz=by)
    own_colour = (own_x + 2 * own_z) % 4
    source_z = own_z + jnp.where((colour - own_colour) % 4 == 2, jnp.where(mine < 2, 1, -1), 0)
    away = (z - source_z) % NZ
    part_rows = got[0]
    for by in (1, 2, -1):
        part_rows = jnp.where(per_round(away == by % NZ), got[by], part_rows)

    near = (away <= 2) | (away == 7)
    part_rows = jnp.where(per_round(near), part_rows, shift(part_rows, dz=4))
    part_rows = jnp.where(per_round(same_y), part_rows, shift(part_rows, dy=1))

    whole = [(mine, part_rows)]
    for by in (1, 2, -1):
        whole.append(((z - by) % 4, shift(part_rows, dx=(-2 * by) % 4, dz=by)))
    mine_rows = jnp.zeros((rounds, 4, part) + tail, gradients.dtype)
    for at, rows in whole:
        mine_rows = lax.dynamic_update_index_in_dim(mine_rows, rows, at, 1)
    mine_rows = mine_rows.reshape(rounds, quarter, *tail)

    half = quarter // 2
    low = shift(mine_rows[:, :half], dz=1)
    high = shift(mine_rows[:, half:], dz=-1)
    before = shift(mine_rows, dx=1)
    after = shift(mine_rows, dx=-1)
    return mine_rows, before, after, jnp.concatenate([low, high], axis=1)


def whiten(rows, whitener):
    count, layers, proj = rows.shape
    nblock, block = whitener.shape[1:3]
    split = rows.reshape(count, layers, nblock, block)
    return jnp.einsum("elbj,lbij->elbi", split, whitener, preferred_element_type=jnp.float32)


def swap(value, axis):
    return lax.ppermute(value, axis, [(0, 1), (1, 0)])


def local(gradients, whitener, owners, query_ids):
    count, layers, proj = gradients.shape
    rounds, queries = query_ids.shape
    colour = (lax.axis_index("x") + 2 * lax.axis_index("z")) % 4
    groups = broadcast(gradients, owners, query_ids)

    whitened = whiten(gradients, whitener)
    norms = jnp.sum(whitened * whitened, axis=(1, 2, 3))
    white_rows = whitened.astype(jnp.bfloat16).reshape(count, layers * proj)
    norms = norms + swap(norms, "core")
    norms = norms + swap(norms, "ylo")

    raw = jnp.stack([groups[0], groups[2], groups[3], groups[1]], axis=1)
    raw = raw.reshape(rounds * queries, layers, proj)
    query = whiten(raw, whitener).astype(jnp.bfloat16).reshape(rounds * queries, layers * proj)
    scores = lax.dot_general(
        query, white_rows, (((1,), (1,)), ((), ())), preferred_element_type=jnp.float32
    )
    scores = scores.reshape(rounds, 4, queries // 4, count)
    scores = jnp.concatenate([scores, scores], axis=1)
    core, ylo = lax.axis_index("core"), lax.axis_index("ylo")

    def colours(which):
        return lax.dynamic_slice_in_dim(scores, (2 * which - colour) % 4, 2, 1)

    half = colours(core) + swap(colours(1 - core), "core")
    mine = lax.dynamic_index_in_dim(half, ylo, 0, keepdims=False)
    mine = mine + swap(lax.dynamic_index_in_dim(half, 1 - ylo, 0, keepdims=False), "ylo")
    mine = mine.reshape(-1, count)
    return mine / jnp.sqrt(norms + 1e-06)[None, :]


def solution(mesh):
    torus = Mesh(mesh.devices.reshape(2, 2, NX, NZ, NY), AXES)
    in_specs = (P(DP, LAYER, None), P(LAYER, None, None, None), P(), P())
    return jax.shard_map(
        local, mesh=torus, in_specs=in_specs, out_specs=P(LAYER, DP), check_vma=False
    )
```

```python
import functools
import itertools

import jax
import jax.numpy as jnp
from jax import lax
from jax.experimental import pallas as pl
from jax.experimental.pallas import tpu as pltpu
from jax.sharding import Mesh
from jax.sharding import PartitionSpec as P

NX, NZ, NY = 4, 8, 2
DP = ("x", "z", "yhi")
LAYER = ("ylo", "core")
AXES = LAYER + DP
SIZES = dict(x=NX, z=NZ, yhi=NY)


def shift(value, dx=0, dz=0, dy=0):
    moves = {name: by for name, by in (("x", dx), ("z", dz), ("yhi", dy)) if by}
    names = tuple(moves)

    def index(place):
        flat = 0
        for name, at in zip(names, place):
            flat = flat * SIZES[name] + at % SIZES[name]
        return flat

    pairs = [
        (index(place), index([at + moves[name] for name, at in zip(names, place)]))
        for place in itertools.product(*(range(SIZES[name]) for name in names))
    ]
    return lax.ppermute(value, names if len(names) > 1 else names[0], pairs)


def pick_kernel(counts, ids, gradients, *rest):
    outs, sem = rest[:-1], rest[-1]
    total = 0
    for out, count in zip(outs, counts):
        base = total

        def start(row, carry, out=out, base=base):
            pltpu.make_async_copy(
                gradients.at[ids[base + row]], out.at[row], sem
            ).start()
            return carry

        lax.fori_loop(0, count, start, 0, unroll=8)
        total += count
    for out, count in zip(outs, counts):
        pltpu.make_async_copy(gradients.at[pl.ds(0, count)], out, sem).wait()


def pick_rows(gradients, ids, counts):
    row = gradients.shape[1:]
    moved = 2 * sum(counts) * row[0] * row[1] * gradients.dtype.itemsize
    return pl.pallas_call(
        functools.partial(pick_kernel, counts),
        out_shape=[jax.ShapeDtypeStruct((n,) + row, gradients.dtype) for n in counts],
        in_specs=[
            pl.BlockSpec(memory_space=pltpu.SMEM),
            pl.BlockSpec(memory_space=pl.ANY),
        ],
        out_specs=[pl.BlockSpec(memory_space=pltpu.VMEM) for _ in counts],
        scratch_shapes=[pltpu.SemaphoreType.DMA],
        cost_estimate=pl.CostEstimate(flops=0, bytes_accessed=moved, transcendentals=0),
    )(ids, gradients)


def per_round(flag):
    return flag.reshape(-1, 1, 1, 1)


def piece(parts, at):
    return lax.dynamic_index_in_dim(parts, at, 1, keepdims=False)


def broadcast(gradients, owners, query_ids, beside):
    rounds, queries = query_ids.shape
    tail = gradients.shape[1:]
    quarter, part = queries // 4, queries // 16
    x, z, y = (lax.axis_index(name) for name in DP)
    colour = (x + 2 * z) % 4
    own_x, own_z, own_y = owners // (NZ * NY), owners // NY % NZ, owners % NY
    far_x, far_z, same_y = (x - own_x) % NX, (z - own_z) % NZ, y == own_y

    by_colour = query_ids.reshape(rounds, 4, quarter)
    order = [by_colour[:, (colour + turn) % 4].reshape(-1) for turn in (0, 1, 3)]
    across = by_colour[:, (colour + 2) % 4]
    order += [across[:, : quarter // 2].reshape(-1), across[:, quarter // 2 :].reshape(-1)]
    counts = tuple(ids.shape[0] for ids in order)
    own, to_right, to_left, to_up, to_down = pick_rows(
        gradients, jnp.concatenate(order), counts
    )
    from_left = shift(to_right, dx=1)
    from_right = shift(to_left, dx=-1)
    from_below = shift(to_up, dz=1)
    from_above = shift(to_down, dz=-1)
    from_left, from_right, from_below, from_above = beside(
        (from_left, from_right, from_below, from_above), to_right
    )
    own, from_left, from_right = (
        rows.reshape(rounds, 4, part, *tail) for rows in (own, from_left, from_right)
    )
    from_below, from_above = (rows.reshape(rounds, 2, part, *tail) for rows in (from_below, from_above))

    def held(at):
        low = at < 2
        out = piece(own, at)
        out = jnp.where(per_round((far_x == 0) & (far_z == 1) & low), piece(from_below, at % 2), out)
        out = jnp.where(per_round((far_x == 0) & (far_z == 7) & ~low), piece(from_above, at % 2), out)
        out = jnp.where(per_round((far_x == 1) & (far_z == 0)), piece(from_left, at), out)
        return jnp.where(per_round((far_x == 3) & (far_z == 0)), piece(from_right, at), out)

    mine = z % 4
    steps = (1, 2, -1)
    pieces = [held((z + by) % 4) for by in steps]
    got = [shift(rows, dx=(-2 * by) % 4, dz=by) for by, rows in zip(steps, pieces)]
    got = dict(zip((0,) + steps, (held(mine),) + tuple(beside(tuple(got), pieces[0]))))
    own_colour = (own_x + 2 * own_z) % 4
    source_z = own_z + jnp.where((colour - own_colour) % 4 == 2, jnp.where(mine < 2, 1, -1), 0)
    away = (z - source_z) % NZ
    part_rows = got[0]
    for by in (1, 2, -1):
        part_rows = jnp.where(per_round(away == by % NZ), got[by], part_rows)

    near = (away <= 2) | (away == 7)
    (moved,) = beside((shift(part_rows, dz=4),), part_rows)
    part_rows = jnp.where(per_round(near), part_rows, moved)
    part_rows = jnp.where(per_round(same_y), part_rows, shift(part_rows, dy=1))

    whole = [(mine, part_rows)]
    for by in steps:
        whole.append(((z - by) % 4, shift(part_rows, dx=(-2 * by) % 4, dz=by)))
    mine_rows = jnp.zeros((rounds, 4, part) + tail, gradients.dtype)
    for at, rows in whole:
        mine_rows = lax.dynamic_update_index_in_dim(mine_rows, rows, at, 1)
    mine_rows = mine_rows.reshape(rounds, quarter, *tail)

    half = quarter // 2
    before, after = shift(mine_rows, dx=1), shift(mine_rows, dx=-1)
    low, high = shift(mine_rows[:, :half], dz=1), shift(mine_rows[:, half:], dz=-1)
    after, low, high, before = beside((after, low, high, before), mine_rows)
    return mine_rows, after, low, high, before


NT = (((1,), (1,)), ((), ()))
VMEM_LIMIT = 48 * 2**20


def whiten_kernel(x_ref, w_ref, *refs):
    white_ref, norm_ref = refs[-2:]
    layers, nb, block = w_ref.shape[:3]
    total = jnp.zeros(norm_ref.shape, jnp.float32)
    for layer in range(layers):
        x = x_ref[:, layer, :]
        for b in range(nb):
            y = lax.dot_general(
                w_ref[layer, b], x[:, b * block : (b + 1) * block], NT, preferred_element_type=jnp.float32
            )
            white_ref[layer, b] = y.astype(white_ref.dtype)
            total = total + jnp.sum((y * y).reshape(-1, *total.shape), axis=0)

    @pl.when(pl.program_id(0) == 0)
    def _():
        norm_ref[...] = jnp.zeros_like(norm_ref)

    norm_ref[...] += total


def whiten_blocks(gradients, whitener, white, first, count, nb=2):
    examples, layers, proj = gradients.shape
    nblock, block = whitener.shape[1:3]
    base = first // nb
    cost = pl.CostEstimate(
        flops=2 * layers * count * block * block * examples,
        bytes_accessed=layers * count * block * (4 * examples + 2 * block) * 3,
        transcendentals=0,
    )
    operands, aliases, extra = [gradients, whitener], {}, []
    if white is not None:
        operands.append(white)
        aliases, extra = {2: 0}, [pl.BlockSpec(memory_space=pl.ANY)]
    return pl.pallas_call(
        whiten_kernel,
        grid=(count // nb,),
        out_shape=[
            jax.ShapeDtypeStruct((layers, nblock, block, examples), jnp.bfloat16),
            jax.ShapeDtypeStruct((8, examples), jnp.float32),
        ],
        in_specs=[
            pl.BlockSpec((examples, layers, nb * block), lambda i: (0, 0, base + i)),
            pl.BlockSpec((layers, nb, block, block), lambda i: (0, base + i, 0, 0)),
        ]
        + extra,
        out_specs=[
            pl.BlockSpec((layers, nb, block, examples), lambda i: (0, base + i, 0, 0)),
            pl.BlockSpec((8, examples), lambda i: (0, 0)),
        ],
        input_output_aliases=aliases,
        compiler_params=pltpu.CompilerParams(vmem_limit_bytes=VMEM_LIMIT),
        cost_estimate=cost,
    )(*operands)


def score_kernel(place, *refs):
    *groups, w_ref, white_ref, keep_ref, send_ref, total_ref = refs
    layers, nb, block = w_ref.shape[:3]
    step = pl.program_id(0)

    @pl.when(step == 0)
    def _():
        total_ref[...] = jnp.zeros_like(total_ref)

    rows = jnp.concatenate([g[...].reshape(-1, *g.shape[2:]) for g in groups], axis=0)
    total = jnp.zeros(total_ref.shape, jnp.float32)
    for layer in range(layers):
        x = rows[:, layer, :]
        for b in range(nb):
            query = lax.dot_general(
                x[:, b * block : (b + 1) * block], w_ref[layer, b], NT, preferred_element_type=jnp.float32
            )
            total = total + jnp.dot(
                query.astype(white_ref.dtype), white_ref[layer, b], preferred_element_type=jnp.float32
            )
    total_ref[...] += total

    @pl.when(step == pl.num_programs(0) - 1)
    def _():
        colour, core = place[0], place[1]
        rounds, _, quarter, _ = keep_ref.shape
        half = quarter // 2
        for turn in range(4):
            at = lax.rem(colour + turn, 4)
            for which in range(rounds):
                if turn == 2:
                    low = 2 * 2 * quarter + which * half
                    high = low + rounds * half
                    spans = ((0, low, half), (half, high, half))
                else:
                    spans = ((0, turn * rounds * quarter + which * quarter, quarter),)
                for to, start, length in spans:
                    value = total_ref[start : start + length]
                    for ref, kept in ((keep_ref, True), (send_ref, False)):

                        @pl.when((at // 2 == core) == kept)
                        def _(ref=ref, value=value, to=to, length=length, which=which, at=at):
                            ref[which, at % 2, to : to + length] = value


def score(groups, whitener, white, place, nb=4):
    layers, nblock, block, examples = white.shape
    rounds, quarter = groups[0].shape[:2]
    count = 4 * rounds * quarter
    out = jax.ShapeDtypeStruct((rounds, 2, quarter, examples), jnp.float32)
    out_spec = pl.BlockSpec(out.shape, lambda i: (0, 0, 0, 0))
    cost = pl.CostEstimate(
        flops=2 * layers * nblock * block * count * (block + examples),
        bytes_accessed=2 * layers * nblock * block * (examples + block + count),
        transcendentals=0,
    )
    return pl.pallas_call(
        score_kernel,
        grid=(nblock // nb,),
        out_shape=[out, out],
        in_specs=[pl.BlockSpec(memory_space=pltpu.SMEM)]
        + [pl.BlockSpec(g.shape[:3] + (nb * block,), lambda i: (0, 0, 0, i)) for g in groups]
        + [
            pl.BlockSpec((layers, nb, block, block), lambda i: (0, i, 0, 0)),
            pl.BlockSpec((layers, nb, block, examples), lambda i: (0, i, 0, 0)),
        ],
        out_specs=[out_spec, out_spec],
        scratch_shapes=[pltpu.VMEM((count, examples), jnp.float32)],
        compiler_params=pltpu.CompilerParams(vmem_limit_bytes=VMEM_LIMIT),
        cost_estimate=cost,
    )(place, *groups, whitener, white)


def swap(value, axis):
    return lax.ppermute(value, axis, [(0, 1), (1, 0)])


SHARES = 4


def local(gradients, whitener, owners, query_ids):
    count = gradients.shape[0]
    share = whitener.shape[1] // SHARES
    colour = (lax.axis_index("x") + 2 * lax.axis_index("z")) % 4
    core, ylo = lax.axis_index("core"), lax.axis_index("ylo")
    done = dict(white=None, norms=[])

    def beside(values, sent):
        rows, _ = lax.optimization_barrier((gradients, sent))
        first = len(done["norms"]) * share
        done["white"], norms = whiten_blocks(rows, whitener, done["white"], first, share)
        values, norms = lax.optimization_barrier((values, norms))
        done["norms"].append(norms)
        return values

    groups = broadcast(gradients, owners, query_ids, beside)
    norms = jnp.sum(sum(done["norms"]), axis=0)
    norms = norms + swap(norms, "core")
    norms = norms + swap(norms, "ylo")

    keep, send = score(groups, whitener, done["white"], jnp.stack([colour, core]).astype(jnp.int32))
    half = keep + swap(send, "core")
    mine = lax.dynamic_index_in_dim(half, ylo, 0, keepdims=False)
    mine = mine + swap(lax.dynamic_index_in_dim(half, 1 - ylo, 0, keepdims=False), "ylo")
    return mine.reshape(-1, count) / jnp.sqrt(norms + 1e-06)[None, :]


def solution(mesh):
    torus = Mesh(mesh.devices.reshape(2, 2, NX, NZ, NY), AXES)
    in_specs = (P(DP, LAYER, None), P(LAYER, None, None, None), P(), P())
    return jax.shard_map(
        local, mesh=torus, in_specs=in_specs, out_specs=P(LAYER, DP), check_vma=False
    )
```

```python
import functools
import itertools

import jax
import jax.numpy as jnp
from jax import lax
from jax.experimental import pallas as pl
from jax.experimental.pallas import tpu as pltpu
from jax.sharding import Mesh
from jax.sharding import PartitionSpec as P

NX, NZ, NY = 4, 8, 2
DP = ("x", "z", "yhi")
LAYER = ("ylo", "core")
AXES = LAYER + DP
SIZES = dict(x=NX, z=NZ, yhi=NY)
NT = (((1,), (1,)), ((), ()))
STEPS = (1, 2, -1)
SMALL_LIMIT, SCORE_LIMIT, LARGE_LIMIT = 8 * 2**20, 40 * 2**20, 57 * 2**20
IN_VMEM = pl.BlockSpec(memory_space=pltpu.VMEM)
IN_SMEM = pl.BlockSpec(memory_space=pltpu.SMEM)


def shift(value, dx=0, dz=0, dy=0):
    moves = {name: by for name, by in (("x", dx), ("z", dz), ("yhi", dy)) if by}
    names = tuple(moves)

    def index(place):
        flat = 0
        for name, at in zip(names, place):
            flat = flat * SIZES[name] + at % SIZES[name]
        return flat

    pairs = [
        (index(place), index([at + moves[name] for name, at in zip(names, place)]))
        for place in itertools.product(*(range(SIZES[name]) for name in names))
    ]
    return lax.ppermute(value, names if len(names) > 1 else names[0], pairs)


def swap(value, axis):
    return lax.ppermute(value, axis, [(0, 1), (1, 0)])


def pick_kernel(turns, place, ids, gradients, *rest):
    outs, sem = rest[:-1], rest[-1]
    rounds, queries = ids.shape
    quarter = queries // 4
    for turn, out in zip(turns, outs):
        first = lax.rem(place[0] + turn, 4) * quarter
        for which in range(rounds):
            for row in range(quarter):
                pltpu.make_async_copy(
                    gradients.at[ids[which, first + row]], out.at[which * quarter + row], sem
                ).start()
    for out in outs:
        pltpu.make_async_copy(gradients.at[pl.ds(0, out.shape[0])], out, sem).wait()


def pick_rows(gradients, query_ids, place, turns):
    count = query_ids.size // 4
    out = jax.ShapeDtypeStruct((count,) + gradients.shape[1:], gradients.dtype)
    moved = 2 * len(turns) * out.size * 2
    return pl.pallas_call(
        functools.partial(pick_kernel, turns),
        out_shape=[out for _ in turns],
        in_specs=[IN_SMEM, IN_SMEM, pl.BlockSpec(memory_space=pl.ANY)],
        out_specs=[IN_VMEM for _ in turns],
        scratch_shapes=[pltpu.SemaphoreType.DMA],
        compiler_params=pltpu.CompilerParams(vmem_limit_bytes=LARGE_LIMIT),
        cost_estimate=pl.CostEstimate(flops=0, bytes_accessed=moved, transcendentals=0),
    )(place, query_ids, gradients)


def split_kernel(same, rows_ref, other_ref, piece_ref, whole_ref):
    rounds, part, layers, _ = rows_ref.shape
    for which in range(rounds):
        keep = same[which] > 0
        for layer in range(layers):
            value = jnp.where(keep, rows_ref[which, :, layer, :], other_ref[which, :, layer, :])
            piece_ref[layer, which * part : (which + 1) * part] = value
            whole_ref[0, layer, which * part : (which + 1) * part] = value


def split_layers(same, rows, other):
    rounds, part, layers, proj = rows.shape
    piece = (layers, rounds * part, proj)
    return pl.pallas_call(
        split_kernel,
        out_shape=[
            jax.ShapeDtypeStruct(piece, rows.dtype),
            jax.ShapeDtypeStruct((4,) + piece, rows.dtype),
        ],
        in_specs=[IN_SMEM, IN_VMEM, IN_VMEM],
        out_specs=[IN_VMEM, IN_VMEM],
        compiler_params=pltpu.CompilerParams(vmem_limit_bytes=SMALL_LIMIT),
        cost_estimate=pl.CostEstimate(flops=0, bytes_accessed=8 * rows.size, transcendentals=0),
    )(same, rows, other)


def per_round(flag):
    return flag.reshape(-1, 1, 1, 1)


def piece(parts, at):
    return lax.dynamic_index_in_dim(parts, at, 1, keepdims=False)


def broadcast(gradients, owners, query_ids, place, beside):
    rounds, queries = query_ids.shape
    tail = gradients.shape[1:]
    part = queries // 16
    x, z, y = (lax.axis_index(name) for name in DP)
    colour = (x + 2 * z) % 4
    own_x, own_z, own_y = owners // (NZ * NY), owners // NY % NZ, owners % NY
    far_x, far_z, same_y = (x - own_x) % NX, (z - own_z) % NZ, y == own_y

    to_right, to_left, to_up = pick_rows(gradients, query_ids, place, (1, 3, 2))
    given = shift(to_right, dx=1), shift(to_left, dx=-1), shift(to_up, dz=1)
    rows, _ = lax.optimization_barrier((gradients, to_up))
    (own,) = pick_rows(rows, query_ids, place, (0,))
    given = beside(given, own, 2)
    own, from_left, from_right, from_below = (
        rows.reshape(rounds, 4, part, *tail) for rows in (own,) + tuple(given)
    )

    def held(at):
        out = jnp.where(per_round((far_x == 0) & (far_z == 1)), piece(from_below, at), piece(own, at))
        out = jnp.where(per_round((far_x == 1) & (far_z == 0)), piece(from_left, at), out)
        return jnp.where(per_round((far_x == 3) & (far_z == 0)), piece(from_right, at), out)

    mine = z % 4
    pieces = [held((z + by) % 4) for by in STEPS]
    got = [shift(rows, dx=(-2 * by) % 4, dz=by) for by, rows in zip(STEPS, pieces)]
    got = beside(tuple(got), pieces[0], 2)
    own_colour = (own_x + 2 * own_z) % 4
    source_z = own_z + jnp.where((colour - own_colour) % 4 == 2, 1, 0)
    away = (z - source_z) % NZ
    part_rows = held(mine)
    for by, rows in zip(STEPS, got):
        part_rows = jnp.where(per_round(away == by % NZ), rows, part_rows)

    near = (away <= 2) | (away == 7)
    (moved,) = beside((shift(part_rows, dz=4),), part_rows, 2)
    part_rows = jnp.where(per_round(near), part_rows, moved)
    (moved,) = beside((shift(part_rows, dy=1),), part_rows, 1)
    mine_rows, whole = split_layers(same_y.astype(jnp.int32), part_rows, moved)

    got = [shift(mine_rows, dx=(-2 * by) % 4, dz=by) for by in STEPS]
    got = beside(tuple(got), mine_rows, 1)
    for at, rows in enumerate(got):
        whole = lax.dynamic_update_index_in_dim(whole, rows, at + 1, 0)

    return whole, shift(whole, dx=-1), shift(whole, dz=1), shift(whole, dx=1)


def whiten_kernel(x_ref, w_ref, *refs):
    white_ref, norm_ref = refs[-2:]
    layers, nb, block = w_ref.shape[:3]
    total = jnp.zeros(norm_ref.shape, jnp.float32)
    for b in range(nb):
        for layer in range(layers):
            y = lax.dot_general(
                w_ref[layer, b],
                x_ref[:, layer, b * block : (b + 1) * block],
                NT,
                preferred_element_type=jnp.float32,
            )
            white_ref[layer, b] = y.astype(white_ref.dtype)
            total = total + jnp.sum((y * y).reshape(-1, *total.shape), axis=0)

    @pl.when(pl.program_id(0) == 0)
    def _():
        norm_ref[...] = jnp.zeros_like(norm_ref)

    norm_ref[...] += total


def whiten_blocks(gradients, whitener, white, first, count, nb=2):
    examples, layers, proj = gradients.shape
    nblock, block = whitener.shape[1:3]
    base = first // nb
    cost = pl.CostEstimate(
        flops=2 * layers * count * block * block * examples,
        bytes_accessed=layers * count * block * (4 * examples + 2 * block) * 3,
        transcendentals=0,
    )
    operands, aliases, extra = [gradients, whitener], {}, []
    if white is not None:
        operands.append(white)
        aliases, extra = {2: 0}, [pl.BlockSpec(memory_space=pl.ANY)]
    return pl.pallas_call(
        whiten_kernel,
        grid=(count // nb,),
        out_shape=[
            jax.ShapeDtypeStruct((layers, nblock, block, examples), jnp.bfloat16),
            jax.ShapeDtypeStruct((8, examples), jnp.float32),
        ],
        in_specs=[
            pl.BlockSpec((examples, layers, nb * block), lambda i: (0, 0, base + i)),
            pl.BlockSpec((layers, nb, block, block), lambda i: (0, base + i, 0, 0)),
        ]
        + extra,
        out_specs=[
            pl.BlockSpec((layers, nb, block, examples), lambda i: (0, base + i, 0, 0)),
            pl.BlockSpec((8, examples), lambda i: (0, 0)),
        ],
        input_output_aliases=aliases,
        compiler_params=pltpu.CompilerParams(vmem_limit_bytes=LARGE_LIMIT),
        cost_estimate=cost,
    )(*operands)


def score_kernel(place, *refs):
    groups, (w_ref, white_ref, keep_ref, send_ref, total_ref) = refs[:4], refs[4:]
    layers, nb, block = w_ref.shape[:3]
    step = pl.program_id(0)

    @pl.when(step == 0)
    def _():
        total_ref[...] = jnp.zeros_like(total_ref)

    total = jnp.zeros(total_ref.shape, jnp.float32)
    for layer in range(layers):
        rows = jnp.concatenate([g[:, layer].reshape(-1, g.shape[-1]) for g in groups], axis=0)
        query = [
            lax.dot_general(
                rows[:, b * block : (b + 1) * block], w_ref[layer, b], NT, preferred_element_type=jnp.float32
            ).astype(white_ref.dtype)
            for b in range(nb)
        ]
        total = total + jnp.dot(
            jnp.concatenate(query, axis=1),
            white_ref[layer].reshape(nb * block, -1),
            preferred_element_type=jnp.float32,
        )
    total_ref[...] += total

    @pl.when(step == pl.num_programs(0) - 1)
    def _():
        colour, core, z = place[0], place[1], place[2]
        rounds, part = keep_ref.shape[0], keep_ref.shape[3]
        for turn in range(4):
            at = lax.rem(colour + turn, 4)
            from_z = z + 8 - (1 if turn == 2 else 0)
            for ref, kept in ((keep_ref, True), (send_ref, False)):

                @pl.when((at // 2 == core) == kept)
                def _(ref=ref, turn=turn, at=at, from_z=from_z):
                    for slot, back in enumerate((0,) + STEPS):
                        for which in range(rounds):
                            start = ((turn * 4 + slot) * rounds + which) * part
                            to = lax.rem(from_z - back, 4)
                            ref[which, lax.rem(at, 2), to] = total_ref[start : start + part]


def score(groups, whitener, white, place, rounds, nb=8):
    layers, nblock, block, examples = white.shape
    part = groups[0].shape[2] // rounds
    count = 16 * rounds * part
    out = jax.ShapeDtypeStruct((rounds, 2, 4, part, examples), jnp.float32)
    out_spec = pl.BlockSpec(out.shape, lambda i: (0, 0, 0, 0, 0))
    cost = pl.CostEstimate(
        flops=2 * layers * nblock * block * count * (block + examples),
        bytes_accessed=2 * layers * nblock * block * (examples + block + count),
        transcendentals=0,
    )
    return pl.pallas_call(
        score_kernel,
        grid=(nblock // nb,),
        out_shape=[out, out],
        in_specs=[IN_SMEM]
        + [pl.BlockSpec(g.shape[:3] + (nb * block,), lambda i: (0, 0, 0, i)) for g in groups]
        + [
            pl.BlockSpec((layers, nb, block, block), lambda i: (0, i, 0, 0)),
            pl.BlockSpec((layers, nb, block, examples), lambda i: (0, i, 0, 0)),
        ],
        out_specs=[out_spec, out_spec],
        scratch_shapes=[pltpu.VMEM((count, examples), jnp.float32)],
        compiler_params=pltpu.CompilerParams(vmem_limit_bytes=SCORE_LIMIT),
        cost_estimate=cost,
    )(place, *groups, whitener, white)


UNITS = 8


def local(gradients, whitener, owners, query_ids):
    count = gradients.shape[0]
    rounds = owners.shape[0]
    unit = whitener.shape[1] // UNITS
    x, z = lax.axis_index("x"), lax.axis_index("z")
    core, ylo = lax.axis_index("core"), lax.axis_index("ylo")
    place = jnp.stack([(x + 2 * z) % 4, core, z]).astype(jnp.int32)
    norms, done = [], dict(units=0, white=None)

    def beside(values, sent, units):
        rows, _ = lax.optimization_barrier((gradients, sent))
        done["white"], norm = whiten_blocks(
            rows, whitener, done["white"], done["units"] * unit, units * unit
        )
        values, norm = lax.optimization_barrier((values, norm))
        norms.append(norm)
        done["units"] += units
        return values

    groups = broadcast(gradients, owners, query_ids, place, beside)
    norm, _ = lax.optimization_barrier((jnp.sum(sum(norms), axis=0), groups[0]))
    norm = norm + swap(norm, "core")
    norm = norm + swap(norm, "ylo")
    groups, norm = lax.optimization_barrier((groups, norm))

    keep, send = score(groups, whitener, done["white"], place, rounds)
    half = keep + swap(send, "core")
    mine = lax.dynamic_index_in_dim(half, ylo, 0, keepdims=False)
    mine = mine + swap(lax.dynamic_index_in_dim(half, 1 - ylo, 0, keepdims=False), "ylo")
    return mine.reshape(-1, count) / jnp.sqrt(norm + 1e-06)[None, :]


def solution(mesh):
    torus = Mesh(mesh.devices.reshape(2, 2, NX, NZ, NY), AXES)
    in_specs = (P(DP, LAYER, None), P(LAYER, None, None, None), P(), P())
    return jax.shard_map(
        local, mesh=torus, in_specs=in_specs, out_specs=P(LAYER, DP), check_vma=False
    )
```

```python
import functools
import itertools

import jax
import jax.numpy as jnp
from jax import lax
from jax.experimental import pallas as pl
from jax.experimental.pallas import tpu as pltpu
from jax.sharding import Mesh
from jax.sharding import PartitionSpec as P

NX, NZ, NY = 4, 8, 2
DP = ("x", "z", "yhi")
LAYER = ("ylo", "core")
AXES = LAYER + DP
SIZES = dict(x=NX, z=NZ, yhi=NY)
NT = (((1,), (1,)), ((), ()))
STEPS = (1, 2, -1)
SMALL_LIMIT, SCORE_LIMIT, LARGE_LIMIT = 8 * 2**20, 26 * 2**20, 57 * 2**20
PICK_LIMIT, STAGE_LIMIT = 52 * 2**20, 24 * 2**20
IN_VMEM = pl.BlockSpec(memory_space=pltpu.VMEM)
IN_SMEM = pl.BlockSpec(memory_space=pltpu.SMEM)


def shift(value, dx=0, dz=0, dy=0):
    moves = {name: by for name, by in (("x", dx), ("z", dz), ("yhi", dy)) if by}
    names = tuple(moves)

    def index(place):
        flat = 0
        for name, at in zip(names, place):
            flat = flat * SIZES[name] + at % SIZES[name]
        return flat

    pairs = [
        (index(place), index([at + moves[name] for name, at in zip(names, place)]))
        for place in itertools.product(*(range(SIZES[name]) for name in names))
    ]
    return lax.ppermute(value, names if len(names) > 1 else names[0], pairs)


def swap(value, axis):
    return lax.ppermute(value, axis, [(0, 1), (1, 0)])


def colour_here():
    return lax.rem(lax.axis_index("x") + 2 * lax.axis_index("z"), 4)


def pick_kernel(wanted, ids, gradients, *rest):
    outs, sem = rest[:-1], rest[-1]
    rounds, queries = ids.shape
    quarter = queries // 4
    colour = colour_here()
    for (turn, skip), out in zip(wanted, outs):
        count = out.shape[0] // rounds
        first = lax.rem(colour + turn, 4) * quarter + skip * count
        for which in range(rounds):
            for row in range(count):
                pltpu.make_async_copy(
                    gradients.at[ids[which, first + row]], out.at[which * count + row], sem
                ).start()
    for out in outs:
        pltpu.make_async_copy(gradients.at[pl.ds(0, out.shape[0])], out, sem).wait()


def pick_rows(gradients, query_ids, wanted, limit=PICK_LIMIT):
    outs = [
        jax.ShapeDtypeStruct((query_ids.size // 4 // parts,) + gradients.shape[1:], gradients.dtype)
        for _, _, parts in wanted
    ]
    return pl.pallas_call(
        functools.partial(pick_kernel, tuple(entry[:2] for entry in wanted)),
        out_shape=outs,
        in_specs=[IN_SMEM, pl.BlockSpec(memory_space=pl.ANY)],
        out_specs=[IN_VMEM for _ in wanted],
        scratch_shapes=[pltpu.SemaphoreType.DMA],
        compiler_params=pltpu.CompilerParams(vmem_limit_bytes=limit),
        cost_estimate=pl.CostEstimate(
            flops=0, bytes_accessed=4 * sum(out.size for out in outs), transcendentals=0
        ),
    )(query_ids, gradients)


def split_kernel(same, rows_ref, other_ref, piece_ref, whole_ref):
    rounds, part, layers, _ = rows_ref.shape
    for which in range(rounds):
        keep = same[which] > 0
        for layer in range(layers):
            value = jnp.where(keep, rows_ref[which, :, layer, :], other_ref[which, :, layer, :])
            piece_ref[layer, which * part : (which + 1) * part] = value
            whole_ref[0, layer, which * part : (which + 1) * part] = value


def split_layers(same, rows, other):
    rounds, part, layers, proj = rows.shape
    piece = (layers, rounds * part, proj)
    return pl.pallas_call(
        split_kernel,
        out_shape=[
            jax.ShapeDtypeStruct(piece, rows.dtype),
            jax.ShapeDtypeStruct((4,) + piece, rows.dtype),
        ],
        in_specs=[IN_SMEM, IN_VMEM, IN_VMEM],
        out_specs=[IN_VMEM, IN_VMEM],
        compiler_params=pltpu.CompilerParams(vmem_limit_bytes=SMALL_LIMIT),
        cost_estimate=pl.CostEstimate(flops=0, bytes_accessed=8 * rows.size, transcendentals=0),
    )(same, rows, other)


def per_round(flag):
    return flag.reshape(-1, 1, 1, 1)


def piece(parts, at):
    return lax.dynamic_index_in_dim(parts, at, 1, keepdims=False)


def broadcast(gradients, owners, query_ids, beside):
    rounds, queries = query_ids.shape
    tail = gradients.shape[1:]
    part = queries // 16
    x, z, y = (lax.axis_index(name) for name in DP)
    colour = (x + 2 * z) % 4
    own_x, own_z, own_y = owners // (NZ * NY), owners // NY % NZ, owners % NY
    far_x, far_z, same_y = (x - own_x) % NX, (z - own_z) % NZ, y == own_y

    to_right, to_left = pick_rows(gradients, query_ids, ((1, 0, 1), (3, 0, 1)))
    given = shift(to_right, dx=1), shift(to_left, dx=-1)
    rows, _ = lax.optimization_barrier((gradients, to_left))
    to_up, to_down, own = pick_rows(rows, query_ids, ((2, 0, 2), (2, 1, 2), (0, 0, 1)), LARGE_LIMIT)
    given += shift(to_up, dz=1), shift(to_down, dz=-1)
    given = beside(given, own, 2)
    own, from_left, from_right, from_below, from_above = (
        rows.reshape(rounds, -1, part, *tail) for rows in (own,) + tuple(given)
    )

    def held(at):
        low = at < 2
        out = piece(own, at)
        out = jnp.where(per_round((far_x == 0) & (far_z == 1) & low), piece(from_below, at % 2), out)
        out = jnp.where(per_round((far_x == 0) & (far_z == 7) & ~low), piece(from_above, at % 2), out)
        out = jnp.where(per_round((far_x == 1) & (far_z == 0)), piece(from_left, at), out)
        return jnp.where(per_round((far_x == 3) & (far_z == 0)), piece(from_right, at), out)

    mine = z % 4
    pieces = [held((z + by) % 4) for by in STEPS]
    got = [shift(rows, dx=(-2 * by) % 4, dz=by) for by, rows in zip(STEPS, pieces)]
    got = beside(tuple(got), pieces[0], 2)
    own_colour = (own_x + 2 * own_z) % 4
    source_z = own_z + jnp.where((colour - own_colour) % 4 == 2, jnp.where(mine < 2, 1, -1), 0)
    away = (z - source_z) % NZ
    part_rows = held(mine)
    for by, rows in zip(STEPS, got):
        part_rows = jnp.where(per_round(away == by % NZ), rows, part_rows)

    near = (away <= 2) | (away == 7)
    (moved,) = beside((shift(part_rows, dz=4),), part_rows, 2)
    part_rows = jnp.where(per_round(near), part_rows, moved)
    (moved,) = beside((shift(part_rows, dy=1),), part_rows, 1)
    mine_rows, whole = split_layers(same_y.astype(jnp.int32), part_rows, moved)

    got = [shift(mine_rows, dx=(-2 * by) % 4, dz=by) for by in STEPS]
    got = beside(tuple(got), mine_rows, 1)
    for at, rows in enumerate(got):
        whole = lax.dynamic_update_index_in_dim(whole, rows, at + 1, 0)

    return whole, shift(whole, dx=-1), shift(whole, dz=1), shift(whole, dx=1)


def whiten_kernel(x_ref, w_ref, *refs):
    white_ref, norm_ref = refs[-2:]
    layers, nb, block = w_ref.shape[:3]
    total = jnp.zeros(norm_ref.shape, jnp.float32)
    for b in range(nb):
        for layer in range(layers):
            y = lax.dot_general(
                w_ref[layer, b],
                x_ref[:, layer, b * block : (b + 1) * block],
                NT,
                preferred_element_type=jnp.float32,
            )
            white_ref[layer, b] = y.astype(white_ref.dtype)
            total = total + jnp.sum((y * y).reshape(-1, *total.shape), axis=0)

    @pl.when(pl.program_id(0) == 0)
    def _():
        norm_ref[...] = jnp.zeros_like(norm_ref)

    norm_ref[...] += total


def whiten_blocks(gradients, whitener, white, first, count, nb=2):
    examples, layers, proj = gradients.shape
    nblock, block = whitener.shape[1:3]
    base = first // nb
    cost = pl.CostEstimate(
        flops=2 * layers * count * block * block * examples,
        bytes_accessed=layers * count * block * (4 * examples + 2 * block) * 3,
        transcendentals=0,
    )
    operands, aliases, extra = [gradients, whitener], {}, []
    if white is not None:
        operands.append(white)
        aliases, extra = {2: 0}, [pl.BlockSpec(memory_space=pl.ANY)]
    return pl.pallas_call(
        whiten_kernel,
        grid=(count // nb,),
        out_shape=[
            jax.ShapeDtypeStruct((layers, nblock, block, examples), jnp.bfloat16),
            jax.ShapeDtypeStruct((8, examples), jnp.float32),
        ],
        in_specs=[
            pl.BlockSpec((examples, layers, nb * block), lambda i: (0, 0, base + i)),
            pl.BlockSpec((layers, nb, block, block), lambda i: (0, base + i, 0, 0)),
        ]
        + extra,
        out_specs=[
            pl.BlockSpec((layers, nb, block, examples), lambda i: (0, base + i, 0, 0)),
            pl.BlockSpec((8, examples), lambda i: (0, 0)),
        ],
        input_output_aliases=aliases,
        compiler_params=pltpu.CompilerParams(vmem_limit_bytes=LARGE_LIMIT),
        cost_estimate=cost,
    )(*operands)


def stage_kernel(white, out, sem):
    copy = pltpu.make_async_copy(white, out, sem)
    copy.start()
    copy.wait()


def stage(white):
    return pl.pallas_call(
        stage_kernel,
        out_shape=jax.ShapeDtypeStruct(white.shape, white.dtype),
        in_specs=[pl.BlockSpec(memory_space=pl.ANY)],
        out_specs=IN_VMEM,
        scratch_shapes=[pltpu.SemaphoreType.DMA],
        compiler_params=pltpu.CompilerParams(vmem_limit_bytes=STAGE_LIMIT),
        cost_estimate=pl.CostEstimate(flops=0, bytes_accessed=4 * white.size, transcendentals=0),
    )(white)


def score_kernel(*refs):
    groups, (w_ref, white_ref, keep_ref, send_ref, total_ref) = refs[:4], refs[4:]
    layers, nb, block = w_ref.shape[:3]
    step = pl.program_id(0)

    @pl.when(step == 0)
    def _():
        total_ref[...] = jnp.zeros_like(total_ref)

    total = jnp.zeros(total_ref.shape, jnp.float32)
    for layer in range(layers):
        rows = jnp.concatenate([g[:, layer].reshape(-1, g.shape[-1]) for g in groups], axis=0)
        query = [
            lax.dot_general(
                rows[:, b * block : (b + 1) * block], w_ref[layer, b], NT, preferred_element_type=jnp.float32
            ).astype(white_ref.dtype)
            for b in range(nb)
        ]
        total = total + jnp.dot(
            jnp.concatenate(query, axis=1),
            white_ref[layer].reshape(nb * block, -1),
            preferred_element_type=jnp.float32,
        )
    total_ref[...] += total

    @pl.when(step == pl.num_programs(0) - 1)
    def _():
        colour, z = colour_here(), lax.axis_index("z")
        core, ylo = lax.axis_index("core"), lax.axis_index("ylo")
        rounds, part = keep_ref.shape[0], keep_ref.shape[3]
        for turn in range(4):
            at = lax.rem(colour + turn, 4)
            from_z = z + 8 - (1 if turn == 2 else 0)
            for ref, kept in ((keep_ref, True), (send_ref, False)):

                @pl.when((at // 2 == core) == kept)
                def _(ref=ref, turn=turn, at=at, from_z=from_z):
                    for slot, back in enumerate((0,) + STEPS):
                        for which in range(rounds):
                            start = ((turn * 4 + slot) * rounds + which) * part
                            to = lax.rem(from_z - back, 4)
                            ref[lax.rem(which + ylo, 2), lax.rem(at, 2), to] = total_ref[start : start + part]


def score(groups, whitener, white, rounds, nb=8):
    layers, nblock, block, examples = white.shape
    part = groups[0].shape[2] // rounds
    count = 16 * rounds * part
    out = jax.ShapeDtypeStruct((rounds, 2, 4, part, examples), jnp.float32)
    out_spec = pl.BlockSpec(out.shape, lambda i: (0, 0, 0, 0, 0))
    cost = pl.CostEstimate(
        flops=2 * layers * nblock * block * count * (block + examples),
        bytes_accessed=2 * layers * nblock * block * (examples + block + count),
        transcendentals=0,
    )
    return pl.pallas_call(
        score_kernel,
        grid=(nblock // nb,),
        out_shape=[out, out],
        in_specs=[pl.BlockSpec(g.shape[:3] + (nb * block,), lambda i: (0, 0, 0, i)) for g in groups]
        + [
            pl.BlockSpec((layers, nb, block, block), lambda i: (0, i, 0, 0)),
            pl.BlockSpec((layers, nb, block, examples), lambda i: (0, i, 0, 0)),
        ],
        out_specs=[out_spec, out_spec],
        scratch_shapes=[pltpu.VMEM((count, examples), jnp.float32)],
        compiler_params=pltpu.CompilerParams(vmem_limit_bytes=SCORE_LIMIT),
        cost_estimate=cost,
    )(*groups, whitener, white)


UNITS = 8


def local(gradients, whitener, owners, query_ids):
    count = gradients.shape[0]
    rounds = owners.shape[0]
    unit = whitener.shape[1] // UNITS
    norms, done = [], dict(units=0, white=None)

    def beside(values, sent, units):
        rows, _ = lax.optimization_barrier((gradients, sent))
        done["white"], norm = whiten_blocks(
            rows, whitener, done["white"], done["units"] * unit, units * unit
        )
        values, norm = lax.optimization_barrier((values, norm))
        norms.append(norm)
        done["units"] += units
        return values

    groups = broadcast(gradients, owners, query_ids, beside)
    norm, _ = lax.optimization_barrier((jnp.sum(sum(norms), axis=0), groups[0]))
    white, _ = lax.optimization_barrier((done["white"], norm))
    norm, white = lax.optimization_barrier((norm + swap(norm, "core"), stage(white)))
    norm = norm + swap(norm, "ylo")
    groups, norm = lax.optimization_barrier((groups, norm))

    keep, send = score(groups, whitener, white, rounds)
    got = swap(send, "core")
    mine = keep[0] + got[0] + swap(keep[1] + got[1], "ylo")
    return mine.reshape(-1, count) / jnp.sqrt(norm + 1e-06)[None, :]


def solution(mesh):
    torus = Mesh(mesh.devices.reshape(2, 2, NX, NZ, NY), AXES)
    in_specs = (P(DP, LAYER, None), P(LAYER, None, None, None), P(), P())
    return jax.shard_map(
        local, mesh=torus, in_specs=in_specs, out_specs=P(LAYER, DP), check_vma=False
    )
```

```python
import functools
import itertools

import jax
import jax.numpy as jnp
from jax import lax
from jax.experimental import pallas as pl
from jax.experimental.pallas import tpu as pltpu
from jax.sharding import Mesh
from jax.sharding import PartitionSpec as P

NX, NZ, NY = 4, 8, 2
DP = ("x", "z", "yhi")
LAYER = ("ylo", "core")
AXES = LAYER + DP
SIZES = dict(x=NX, z=NZ, yhi=NY)
NT = (((1,), (1,)), ((), ()))
STEPS = (1, 2, -1)
SMALL_LIMIT, SCORE_LIMIT, LARGE_LIMIT = 8 * 2**20, 26 * 2**20, 57 * 2**20
PICK_LIMIT, STAGE_LIMIT = 52 * 2**20, 24 * 2**20
IN_VMEM = pl.BlockSpec(memory_space=pltpu.VMEM)
IN_SMEM = pl.BlockSpec(memory_space=pltpu.SMEM)


def shift(value, dx=0, dz=0, dy=0):
    moves = {name: by for name, by in (("x", dx), ("z", dz), ("yhi", dy)) if by}
    names = tuple(moves)

    def index(place):
        flat = 0
        for name, at in zip(names, place):
            flat = flat * SIZES[name] + at % SIZES[name]
        return flat

    pairs = [
        (index(place), index([at + moves[name] for name, at in zip(names, place)]))
        for place in itertools.product(*(range(SIZES[name]) for name in names))
    ]
    return lax.ppermute(value, names if len(names) > 1 else names[0], pairs)


def swap(value, axis):
    return lax.ppermute(value, axis, [(0, 1), (1, 0)])


def colour_here():
    return lax.rem(lax.axis_index("x") + 2 * lax.axis_index("z"), 4)


def pick_kernel(wanted, ids, gradients, *rest):
    outs, sem = rest[:-1], rest[-1]
    rounds, queries = ids.shape
    quarter = queries // 4
    colour = colour_here()
    for (turn, skip), out in zip(wanted, outs):
        count = out.shape[0] // rounds
        first = lax.rem(colour + turn, 4) * quarter + skip * count
        for which in range(rounds):
            for row in range(count):
                pltpu.make_async_copy(
                    gradients.at[ids[which, first + row]], out.at[which * count + row], sem
                ).start()
    for out in outs:
        pltpu.make_async_copy(gradients.at[pl.ds(0, out.shape[0])], out, sem).wait()


def pick_rows(gradients, query_ids, wanted, limit=PICK_LIMIT):
    outs = [
        jax.ShapeDtypeStruct((query_ids.size // 4 // parts,) + gradients.shape[1:], gradients.dtype)
        for _, _, parts in wanted
    ]
    return pl.pallas_call(
        functools.partial(pick_kernel, tuple(entry[:2] for entry in wanted)),
        out_shape=outs,
        in_specs=[IN_SMEM, pl.BlockSpec(memory_space=pl.ANY)],
        out_specs=[IN_VMEM for _ in wanted],
        scratch_shapes=[pltpu.SemaphoreType.DMA],
        compiler_params=pltpu.CompilerParams(vmem_limit_bytes=limit),
        cost_estimate=pl.CostEstimate(
            flops=0, bytes_accessed=4 * sum(out.size for out in outs), transcendentals=0
        ),
    )(query_ids, gradients)


def split_kernel(same, rows_ref, other_ref, piece_ref, whole_ref):
    rounds, part, layers, _ = rows_ref.shape
    for which in range(rounds):
        keep = same[which] > 0
        for layer in range(layers):
            value = jnp.where(keep, rows_ref[which, :, layer, :], other_ref[which, :, layer, :])
            piece_ref[layer, which * part : (which + 1) * part] = value
            whole_ref[0, layer, which * part : (which + 1) * part] = value


def split_layers(same, rows, other):
    rounds, part, layers, proj = rows.shape
    piece = (layers, rounds * part, proj)
    return pl.pallas_call(
        split_kernel,
        out_shape=[
            jax.ShapeDtypeStruct(piece, rows.dtype),
            jax.ShapeDtypeStruct((4,) + piece, rows.dtype),
        ],
        in_specs=[IN_SMEM, IN_VMEM, IN_VMEM],
        out_specs=[IN_VMEM, IN_VMEM],
        compiler_params=pltpu.CompilerParams(vmem_limit_bytes=SMALL_LIMIT),
        cost_estimate=pl.CostEstimate(flops=0, bytes_accessed=8 * rows.size, transcendentals=0),
    )(same, rows, other)


def per_round(flag):
    return flag.reshape(-1, 1, 1, 1)


def piece(parts, at):
    return lax.dynamic_index_in_dim(parts, at, 1, keepdims=False)


def broadcast(gradients, owners, query_ids, beside):
    rounds, queries = query_ids.shape
    tail = gradients.shape[1:]
    part = queries // 16
    x, z, y = (lax.axis_index(name) for name in DP)
    colour = (x + 2 * z) % 4
    own_x, own_z, own_y = owners // (NZ * NY), owners // NY % NZ, owners % NY
    far_x, far_z, same_y = (x - own_x) % NX, (z - own_z) % NZ, y == own_y

    to_right, to_left = pick_rows(gradients, query_ids, ((1, 0, 1), (3, 0, 1)))
    given = shift(to_right, dx=1), shift(to_left, dx=-1)
    rows, _ = lax.optimization_barrier((gradients, to_left))
    to_up, to_down, own = pick_rows(rows, query_ids, ((2, 0, 2), (2, 1, 2), (0, 0, 1)), LARGE_LIMIT)
    given += shift(to_up, dz=1), shift(to_down, dz=-1)
    given = beside(given, own, 2)
    own, from_left, from_right, from_below, from_above = (
        rows.reshape(rounds, -1, part, *tail) for rows in (own,) + tuple(given)
    )

    def held(at):
        low = at < 2
        out = piece(own, at)
        out = jnp.where(per_round((far_x == 0) & (far_z == 1) & low), piece(from_below, at % 2), out)
        out = jnp.where(per_round((far_x == 0) & (far_z == 7) & ~low), piece(from_above, at % 2), out)
        out = jnp.where(per_round((far_x == 1) & (far_z == 0)), piece(from_left, at), out)
        return jnp.where(per_round((far_x == 3) & (far_z == 0)), piece(from_right, at), out)

    mine = z % 4
    pieces = [held((z + by) % 4) for by in STEPS]
    got = [shift(rows, dx=(-2 * by) % 4, dz=by) for by, rows in zip(STEPS, pieces)]
    got = beside(tuple(got), pieces[0], 2)
    own_colour = (own_x + 2 * own_z) % 4
    source_z = own_z + jnp.where((colour - own_colour) % 4 == 2, jnp.where(mine < 2, 1, -1), 0)
    away = (z - source_z) % NZ
    part_rows = held(mine)
    for by, rows in zip(STEPS, got):
        part_rows = jnp.where(per_round(away == by % NZ), rows, part_rows)

    near = (away <= 2) | (away == 7)
    (moved,) = beside((shift(part_rows, dz=4),), part_rows, 2)
    part_rows = jnp.where(per_round(near), part_rows, moved)
    (moved,) = beside((shift(part_rows, dy=1),), part_rows, 1)
    mine_rows, whole = split_layers(same_y.astype(jnp.int32), part_rows, moved)

    got = [shift(mine_rows, dx=(-2 * by) % 4, dz=by) for by in STEPS]
    got = beside(tuple(got), mine_rows, 1)
    for at, rows in enumerate(got):
        whole = lax.dynamic_update_index_in_dim(whole, rows, at + 1, 0)

    return whole, shift(whole, dx=-1), shift(whole, dz=1), shift(whole, dx=1)


def whiten_kernel(x_ref, w_ref, *refs):
    white_ref, norm_ref = refs[-2:]
    layers, nb, block = w_ref.shape[:3]
    total = jnp.zeros(norm_ref.shape, jnp.float32)
    for b in range(nb):
        for layer in range(layers):
            y = lax.dot_general(
                w_ref[layer, b],
                x_ref[:, layer, b * block : (b + 1) * block],
                NT,
                preferred_element_type=jnp.float32,
            )
            white_ref[layer, b] = y.astype(white_ref.dtype)
            total = total + jnp.sum((y * y).reshape(-1, *total.shape), axis=0)

    @pl.when(pl.program_id(0) == 0)
    def _():
        norm_ref[...] = jnp.zeros_like(norm_ref)

    norm_ref[...] += total


def whiten_blocks(gradients, whitener, white, first, count, nb=2):
    examples, layers, proj = gradients.shape
    nblock, block = whitener.shape[1:3]
    base = first // nb
    cost = pl.CostEstimate(
        flops=2 * layers * count * block * block * examples,
        bytes_accessed=layers * count * block * (4 * examples + 2 * block) * 3,
        transcendentals=0,
    )
    operands, aliases, extra = [gradients, whitener], {}, []
    if white is not None:
        operands.append(white)
        aliases, extra = {2: 0}, [pl.BlockSpec(memory_space=pl.ANY)]
    return pl.pallas_call(
        whiten_kernel,
        grid=(count // nb,),
        out_shape=[
            jax.ShapeDtypeStruct((layers, nblock, block, examples), jnp.bfloat16),
            jax.ShapeDtypeStruct((8, examples), jnp.float32),
        ],
        in_specs=[
            pl.BlockSpec((examples, layers, nb * block), lambda i: (0, 0, base + i)),
            pl.BlockSpec((layers, nb, block, block), lambda i: (0, base + i, 0, 0)),
        ]
        + extra,
        out_specs=[
            pl.BlockSpec((layers, nb, block, examples), lambda i: (0, base + i, 0, 0)),
            pl.BlockSpec((8, examples), lambda i: (0, 0)),
        ],
        input_output_aliases=aliases,
        compiler_params=pltpu.CompilerParams(vmem_limit_bytes=LARGE_LIMIT),
        cost_estimate=cost,
    )(*operands)


def stage_kernel(white, out, sem):
    copy = pltpu.make_async_copy(white, out, sem)
    copy.start()
    copy.wait()


def stage(white):
    return pl.pallas_call(
        stage_kernel,
        out_shape=jax.ShapeDtypeStruct(white.shape, white.dtype),
        in_specs=[pl.BlockSpec(memory_space=pl.ANY)],
        out_specs=IN_VMEM,
        scratch_shapes=[pltpu.SemaphoreType.DMA],
        compiler_params=pltpu.CompilerParams(vmem_limit_bytes=STAGE_LIMIT),
        cost_estimate=pl.CostEstimate(flops=0, bytes_accessed=4 * white.size, transcendentals=0),
    )(white)


def score_kernel(*refs):
    groups, (w_ref, white_ref, keep_ref, send_ref, total_ref) = refs[:4], refs[4:]
    layers, nblock, block = w_ref.shape[:3]
    nb = nblock // 2
    total = jnp.zeros(total_ref.shape, jnp.float32)
    for layer in range(layers):
        for first in range(0, nblock, nb):
            span = slice(first * block, (first + nb) * block)
            rows = jnp.concatenate(
                [g[:, layer, :, span].reshape(-1, nb * block) for g in groups], axis=0
            )
            query = [
                lax.dot_general(
                    rows[:, b * block : (b + 1) * block],
                    w_ref[layer, first + b],
                    NT,
                    preferred_element_type=jnp.float32,
                ).astype(white_ref.dtype)
                for b in range(nb)
            ]
            total = total + jnp.dot(
                jnp.concatenate(query, axis=1),
                white_ref[layer, first : first + nb].reshape(nb * block, -1),
                preferred_element_type=jnp.float32,
            )
    total_ref[...] = total

    colour, z = colour_here(), lax.axis_index("z")
    core, ylo = lax.axis_index("core"), lax.axis_index("ylo")
    rounds, part = keep_ref.shape[0], keep_ref.shape[3]
    for turn in range(4):
        at = lax.rem(colour + turn, 4)
        from_z = z + 8 - (1 if turn == 2 else 0)
        for ref, kept in ((keep_ref, True), (send_ref, False)):

            @pl.when((at // 2 == core) == kept)
            def _(ref=ref, turn=turn, at=at, from_z=from_z):
                for slot, back in enumerate((0,) + STEPS):
                    for which in range(rounds):
                        start = ((turn * 4 + slot) * rounds + which) * part
                        to = lax.rem(from_z - back, 4)
                        ref[lax.rem(which + ylo, 2), lax.rem(at, 2), to] = total_ref[start : start + part]


def score(groups, whitener, white, rounds):
    layers, nblock, block, examples = white.shape
    part = groups[0].shape[2] // rounds
    count = 16 * rounds * part
    out = jax.ShapeDtypeStruct((rounds, 2, 4, part, examples), jnp.float32)
    cost = pl.CostEstimate(
        flops=2 * layers * nblock * block * count * (block + examples),
        bytes_accessed=2 * layers * nblock * block * (examples + block + count),
        transcendentals=0,
    )
    return pl.pallas_call(
        score_kernel,
        out_shape=[out, out],
        in_specs=[IN_VMEM] * (len(groups) + 2),
        out_specs=[IN_VMEM, IN_VMEM],
        scratch_shapes=[pltpu.VMEM((count, examples), jnp.float32)],
        compiler_params=pltpu.CompilerParams(vmem_limit_bytes=SCORE_LIMIT),
        cost_estimate=cost,
    )(*groups, whitener, white)


UNITS = 8


def local(gradients, whitener, owners, query_ids):
    count = gradients.shape[0]
    rounds = owners.shape[0]
    unit = whitener.shape[1] // UNITS
    norms, done = [], dict(units=0, white=None)

    def beside(values, sent, units):
        rows, _ = lax.optimization_barrier((gradients, sent))
        done["white"], norm = whiten_blocks(
            rows, whitener, done["white"], done["units"] * unit, units * unit
        )
        values, norm = lax.optimization_barrier((values, norm))
        norms.append(norm)
        done["units"] += units
        return values

    groups = broadcast(gradients, owners, query_ids, beside)
    norm, _ = lax.optimization_barrier((jnp.sum(sum(norms), axis=0), groups[0]))
    white, _ = lax.optimization_barrier((done["white"], norm))
    norm, white = lax.optimization_barrier((norm + swap(norm, "core"), stage(white)))
    groups, white, norm = lax.optimization_barrier((groups, white, norm))
    norm = norm + swap(norm, "ylo")

    keep, send = score(groups, whitener, white, rounds)
    got = swap(send, "core")
    mine = keep[0] + got[0] + swap(keep[1] + got[1], "ylo")
    return mine.reshape(-1, count) / jnp.sqrt(norm + 1e-06)[None, :]


def solution(mesh):
    torus = Mesh(mesh.devices.reshape(2, 2, NX, NZ, NY), AXES)
    in_specs = (P(DP, LAYER, None), P(LAYER, None, None, None), P(), P())
    return jax.shard_map(
        local, mesh=torus, in_specs=in_specs, out_specs=P(LAYER, DP), check_vma=False
    )
```

```python
import functools
import itertools

import jax
import jax.numpy as jnp
from jax import lax
from jax.experimental import pallas as pl
from jax.experimental.pallas import tpu as pltpu
from jax.sharding import Mesh
from jax.sharding import PartitionSpec as P

NX, NZ, NY = 4, 8, 2
DP = ("x", "z", "yhi")
LAYER = ("ylo", "core")
AXES = LAYER + DP
SIZES = dict(x=NX, z=NZ, yhi=NY)
NT = (((1,), (1,)), ((), ()))
STEPS = (1, 2, -1)
SMALL_LIMIT, SCORE_LIMIT, LARGE_LIMIT = 8 * 2**20, 26 * 2**20, 57 * 2**20
PICK_LIMIT, STAGE_LIMIT = 52 * 2**20, 24 * 2**20
IN_VMEM = pl.BlockSpec(memory_space=pltpu.VMEM)
IN_SMEM = pl.BlockSpec(memory_space=pltpu.SMEM)


def shift(value, dx=0, dz=0, dy=0):
    moves = {name: by for name, by in (("x", dx), ("z", dz), ("yhi", dy)) if by}
    names = tuple(moves)

    def index(place):
        flat = 0
        for name, at in zip(names, place):
            flat = flat * SIZES[name] + at % SIZES[name]
        return flat

    pairs = [
        (index(place), index([at + moves[name] for name, at in zip(names, place)]))
        for place in itertools.product(*(range(SIZES[name]) for name in names))
    ]
    return lax.ppermute(value, names if len(names) > 1 else names[0], pairs)


def swap(value, axis):
    return lax.ppermute(value, axis, [(0, 1), (1, 0)])


def colour_here():
    return lax.rem(lax.axis_index("x") + 2 * lax.axis_index("z"), 4)


def pick_kernel(wanted, ids, gradients, *rest):
    outs, sem = rest[:-1], rest[-1]
    rounds, queries = ids.shape
    quarter = queries // 4
    colour = colour_here()
    for (turn, skip), out in zip(wanted, outs):
        count = out.shape[0] // rounds
        first = lax.rem(colour + turn, 4) * quarter + skip * count
        for which in range(rounds):
            for row in range(count):
                pltpu.make_async_copy(
                    gradients.at[ids[which, first + row]], out.at[which * count + row], sem
                ).start()
    for out in outs:
        pltpu.make_async_copy(gradients.at[pl.ds(0, out.shape[0])], out, sem).wait()


def pick_rows(gradients, query_ids, wanted, limit=PICK_LIMIT):
    outs = [
        jax.ShapeDtypeStruct((query_ids.size // 4 // parts,) + gradients.shape[1:], gradients.dtype)
        for _, _, parts in wanted
    ]
    return pl.pallas_call(
        functools.partial(pick_kernel, tuple(entry[:2] for entry in wanted)),
        out_shape=outs,
        in_specs=[IN_SMEM, pl.BlockSpec(memory_space=pl.ANY)],
        out_specs=[IN_VMEM for _ in wanted],
        scratch_shapes=[pltpu.SemaphoreType.DMA],
        compiler_params=pltpu.CompilerParams(vmem_limit_bytes=limit),
        cost_estimate=pl.CostEstimate(
            flops=0, bytes_accessed=4 * sum(out.size for out in outs), transcendentals=0
        ),
    )(query_ids, gradients)


def split_kernel(same, rows_ref, other_ref, piece_ref, whole_ref):
    rounds, part, layers, _ = rows_ref.shape
    for which in range(rounds):
        keep = same[which] > 0
        for layer in range(layers):
            value = jnp.where(keep, rows_ref[which, :, layer, :], other_ref[which, :, layer, :])
            piece_ref[layer, which * part : (which + 1) * part] = value
            whole_ref[0, layer, which * part : (which + 1) * part] = value


def split_layers(same, rows, other):
    rounds, part, layers, proj = rows.shape
    piece = (layers, rounds * part, proj)
    return pl.pallas_call(
        split_kernel,
        out_shape=[
            jax.ShapeDtypeStruct(piece, rows.dtype),
            jax.ShapeDtypeStruct((4,) + piece, rows.dtype),
        ],
        in_specs=[IN_SMEM, IN_VMEM, IN_VMEM],
        out_specs=[IN_VMEM, IN_VMEM],
        compiler_params=pltpu.CompilerParams(vmem_limit_bytes=SMALL_LIMIT),
        cost_estimate=pl.CostEstimate(flops=0, bytes_accessed=8 * rows.size, transcendentals=0),
    )(same, rows, other)


def per_round(flag):
    return flag.reshape(-1, 1, 1, 1)


def piece(parts, at):
    return lax.dynamic_index_in_dim(parts, at, 1, keepdims=False)


def broadcast(gradients, owners, query_ids, beside):
    rounds, queries = query_ids.shape
    tail = gradients.shape[1:]
    part = queries // 16
    x, z, y = (lax.axis_index(name) for name in DP)
    colour = (x + 2 * z) % 4
    own_x, own_z, own_y = owners // (NZ * NY), owners // NY % NZ, owners % NY
    far_x, far_z, same_y = (x - own_x) % NX, (z - own_z) % NZ, y == own_y

    to_right, to_left = pick_rows(gradients, query_ids, ((1, 0, 1), (3, 0, 1)))
    given = shift(to_right, dx=1), shift(to_left, dx=-1)
    rows, _ = lax.optimization_barrier((gradients, to_left))
    to_up, to_down, own = pick_rows(rows, query_ids, ((2, 0, 2), (2, 1, 2), (0, 0, 1)), LARGE_LIMIT)
    given += shift(to_up, dz=1), shift(to_down, dz=-1)
    given = beside(given, own, 2)
    own, from_left, from_right, from_below, from_above = (
        rows.reshape(rounds, -1, part, *tail) for rows in (own,) + tuple(given)
    )

    def held(at):
        low = at < 2
        out = piece(own, at)
        out = jnp.where(per_round((far_x == 0) & (far_z == 1) & low), piece(from_below, at % 2), out)
        out = jnp.where(per_round((far_x == 0) & (far_z == 7) & ~low), piece(from_above, at % 2), out)
        out = jnp.where(per_round((far_x == 1) & (far_z == 0)), piece(from_left, at), out)
        return jnp.where(per_round((far_x == 3) & (far_z == 0)), piece(from_right, at), out)

    mine = z % 4
    pieces = [held((z + by) % 4) for by in STEPS]
    got = [shift(rows, dx=(-2 * by) % 4, dz=by) for by, rows in zip(STEPS, pieces)]
    got = beside(tuple(got), pieces[0], 2)
    own_colour = (own_x + 2 * own_z) % 4
    source_z = own_z + jnp.where((colour - own_colour) % 4 == 2, jnp.where(mine < 2, 1, -1), 0)
    away = (z - source_z) % NZ
    part_rows = held(mine)
    for by, rows in zip(STEPS, got):
        part_rows = jnp.where(per_round(away == by % NZ), rows, part_rows)

    near = (away <= 2) | (away == 7)
    (moved,) = beside((shift(part_rows, dz=4),), part_rows, 2)
    part_rows = jnp.where(per_round(near), part_rows, moved)
    (moved,) = beside((shift(part_rows, dy=1),), part_rows, 1)
    mine_rows, whole = split_layers(same_y.astype(jnp.int32), part_rows, moved)

    got = [shift(mine_rows, dx=(-2 * by) % 4, dz=by) for by in STEPS]
    got = beside(tuple(got), mine_rows, 1)
    for at, rows in enumerate(got):
        whole = lax.dynamic_update_index_in_dim(whole, rows, at + 1, 0)

    after, before = shift(whole, dx=-1), shift(whole, dx=1)
    return whole, after, shift(whole[:2], dz=1), shift(whole[:2], dz=-1), before


def whiten_kernel(x_ref, w_ref, *refs):
    white_ref, norm_ref = refs[-2:]
    layers, nb, block = w_ref.shape[:3]
    total = jnp.zeros(norm_ref.shape, jnp.float32)
    for b in range(nb):
        for layer in range(layers):
            y = lax.dot_general(
                w_ref[layer, b],
                x_ref[:, layer, b * block : (b + 1) * block],
                NT,
                preferred_element_type=jnp.float32,
            )
            white_ref[layer, b] = y.astype(white_ref.dtype)
            total = total + jnp.sum((y * y).reshape(-1, *total.shape), axis=0)

    @pl.when(pl.program_id(0) == 0)
    def _():
        norm_ref[...] = jnp.zeros_like(norm_ref)

    norm_ref[...] += total


def whiten_blocks(gradients, whitener, white, first, count, nb=2):
    examples, layers, proj = gradients.shape
    nblock, block = whitener.shape[1:3]
    base = first // nb
    cost = pl.CostEstimate(
        flops=2 * layers * count * block * block * examples,
        bytes_accessed=layers * count * block * (4 * examples + 2 * block) * 3,
        transcendentals=0,
    )
    operands, aliases, extra = [gradients, whitener], {}, []
    if white is not None:
        operands.append(white)
        aliases, extra = {2: 0}, [pl.BlockSpec(memory_space=pl.ANY)]
    return pl.pallas_call(
        whiten_kernel,
        grid=(count // nb,),
        out_shape=[
            jax.ShapeDtypeStruct((layers, nblock, block, examples), jnp.bfloat16),
            jax.ShapeDtypeStruct((8, examples), jnp.float32),
        ],
        in_specs=[
            pl.BlockSpec((examples, layers, nb * block), lambda i: (0, 0, base + i)),
            pl.BlockSpec((layers, nb, block, block), lambda i: (0, base + i, 0, 0)),
        ]
        + extra,
        out_specs=[
            pl.BlockSpec((layers, nb, block, examples), lambda i: (0, base + i, 0, 0)),
            pl.BlockSpec((8, examples), lambda i: (0, 0)),
        ],
        input_output_aliases=aliases,
        compiler_params=pltpu.CompilerParams(vmem_limit_bytes=LARGE_LIMIT),
        cost_estimate=cost,
    )(*operands)


def stage_kernel(white, _, out, sem):
    copy = pltpu.make_async_copy(white, out, sem)
    copy.start()
    copy.wait()


def stage(white, whitener):
    return pl.pallas_call(
        stage_kernel,
        out_shape=jax.ShapeDtypeStruct(white.shape, white.dtype),
        in_specs=[pl.BlockSpec(memory_space=pl.ANY), IN_VMEM],
        out_specs=IN_VMEM,
        scratch_shapes=[pltpu.SemaphoreType.DMA],
        compiler_params=pltpu.CompilerParams(vmem_limit_bytes=STAGE_LIMIT),
        cost_estimate=pl.CostEstimate(flops=0, bytes_accessed=4 * white.size, transcendentals=0),
    )(white, whitener)


def score_kernel(*refs):
    groups, (w_ref, white_ref, keep_ref, send_ref, total_ref) = refs[:5], refs[5:]
    layers, nblock, block = w_ref.shape[:3]
    nb = nblock // 2
    total = jnp.zeros(total_ref.shape, jnp.float32)
    for layer in range(layers):
        for first in range(0, nblock, nb):
            span = slice(first * block, (first + nb) * block)
            rows = jnp.concatenate(
                [g[:, layer, :, span].reshape(-1, nb * block) for g in groups], axis=0
            )
            query = [
                lax.dot_general(
                    rows[:, b * block : (b + 1) * block],
                    w_ref[layer, first + b],
                    NT,
                    preferred_element_type=jnp.float32,
                ).astype(white_ref.dtype)
                for b in range(nb)
            ]
            total = total + jnp.dot(
                jnp.concatenate(query, axis=1),
                white_ref[layer, first : first + nb].reshape(nb * block, -1),
                preferred_element_type=jnp.float32,
            )
    total_ref[...] = total

    colour, z = colour_here(), lax.axis_index("z")
    core, ylo = lax.axis_index("core"), lax.axis_index("ylo")
    rounds, part = keep_ref.shape[0], keep_ref.shape[3]
    for turn in range(4):
        at = lax.rem(colour + turn, 4)
        for ref, kept in ((keep_ref, True), (send_ref, False)):

            @pl.when((at // 2 == core) == kept)
            def _(ref=ref, turn=turn, at=at):
                for slot, back in enumerate((1, 2, -1, 0) if turn == 2 else (0,) + STEPS):
                    for which in range(rounds):
                        start = ((turn * 4 + slot) * rounds + which) * part
                        to = lax.rem(z + 8 - back, 4)
                        ref[lax.rem(which + ylo, 2), lax.rem(at, 2), to] = total_ref[start : start + part]


def score(groups, whitener, white, rounds):
    layers, nblock, block, examples = white.shape
    part = groups[0].shape[2] // rounds
    count = 16 * rounds * part
    out = jax.ShapeDtypeStruct((rounds, 2, 4, part, examples), jnp.float32)
    cost = pl.CostEstimate(
        flops=2 * layers * nblock * block * count * (block + examples),
        bytes_accessed=2 * layers * nblock * block * (examples + block + count),
        transcendentals=0,
    )
    return pl.pallas_call(
        score_kernel,
        out_shape=[out, out],
        in_specs=[IN_VMEM] * (len(groups) + 2),
        out_specs=[IN_VMEM, IN_VMEM],
        scratch_shapes=[pltpu.VMEM((count, examples), jnp.float32)],
        compiler_params=pltpu.CompilerParams(vmem_limit_bytes=SCORE_LIMIT),
        cost_estimate=cost,
    )(*groups, whitener, white)


UNITS = 8


def local(gradients, whitener, owners, query_ids):
    count = gradients.shape[0]
    rounds = owners.shape[0]
    unit = whitener.shape[1] // UNITS
    norms, done = [], dict(units=0, white=None)

    def beside(values, sent, units):
        rows, _ = lax.optimization_barrier((gradients, sent))
        done["white"], norm = whiten_blocks(
            rows, whitener, done["white"], done["units"] * unit, units * unit
        )
        values, norm = lax.optimization_barrier((values, norm))
        norms.append(norm)
        done["units"] += units
        return values

    groups = broadcast(gradients, owners, query_ids, beside)
    norm, _ = lax.optimization_barrier((jnp.sum(sum(norms), axis=0), groups[0]))
    white, _ = lax.optimization_barrier((done["white"], norm))
    norm, white = lax.optimization_barrier((norm + swap(norm, "core"), stage(white, whitener)))
    groups, white, norm = lax.optimization_barrier((groups, white, norm))
    norm = norm + swap(norm, "ylo")

    keep, send = score(groups, whitener, white, rounds)
    got = swap(send, "core")
    mine = keep[0] + got[0] + swap(keep[1] + got[1], "ylo")
    return mine.reshape(-1, count) / jnp.sqrt(norm + 1e-06)[None, :]


def solution(mesh):
    torus = Mesh(mesh.devices.reshape(2, 2, NX, NZ, NY), AXES)
    in_specs = (P(DP, LAYER, None), P(LAYER, None, None, None), P(), P())
    return jax.shard_map(
        local, mesh=torus, in_specs=in_specs, out_specs=P(LAYER, DP), check_vma=False
    )
```
